32 devices in a mesh: sta: 2 (over x), gx: 4 (over z), gy: 4 (over y, core).
Axes of the slice: x: 2, y: 2, z: 4, core: 2. Of those that a mesh axis runs over, the one named last changes fastest.
Arguments:
- record: float32 [128, 1024], replicated, may hold values from -6 to 6
- shifts: int32 [128, 256], P(None, 'gx'), may hold values from 0 to 1022
- station_group: int32 [128], replicated, may hold values from 0 to 7
- weights: bfloat16 [128, 256, 512], P('sta', 'gy'), may hold values from -6 to 6
- psf_real: float32 [256, 256, 512], P(None, 'gx', 'gy'), may hold values from -6 to 6
- psf_imag: float32 [256, 256, 512], P(None, 'gx', 'gy'), may hold values from -6 to 6
Outputs:
- image: float32 [2, 256, 256, 512], P('sta', 'gx', 'gy')
The draws below stay inside these ranges and needn't reach their ends.
All inputs are finite; a program needn't handle non-finite values.
Results may differ from the reference program's by a relative error of at most 0.0029.
Values may be sent and summed in bfloat16 or wider, within the bound.
A program may use at most 128 MiB of HBM per device.

```python
import math
import jax
import jax.numpy as jnp
import numpy as np
from jax import lax

STATIONS = 128
TIMES = 2
NZ = 256
NX = 256
NY = 512
TRACE = 1024
GROUPS = 8


def plant(array, stream_key, least, top_value):
    place = [jax.random.randint(jax.random.fold_in(stream_key, axis), (), 0, length) for axis, length in enumerate(array.shape)]
    widest = array.shape.index(max(array.shape))
    beside = place[:widest] + [(place[widest] + 1) % array.shape[widest]] + place[widest + 1:]
    return array.at[tuple(place)].set(least).at[tuple(beside)].set(top_value)


def block_levels(own_key, extent, split, smallest, high):
    factor_of = 1.0
    for position, blocks in split:
        heights = jax.random.uniform(jax.random.fold_in(jax.random.fold_in(own_key, 6), position), (blocks,), jnp.float32, smallest / len(split), high / len(split))
        factor_of = factor_of * jnp.repeat(jnp.exp(heights), extent[position] // blocks).reshape((-1,) + (1,) * (len(extent) - 1 - position))
    return factor_of


def cumulative_ranks(amount, lean):
    weights = [(1 << 20) // math.isqrt(standing ** lean) + 1 for standing in range(1, amount + 1)]
    spread = 1 + sum(weights) // (1 << 30)
    return np.cumsum(np.array([max(1, weight // spread) for weight in weights]))


def skewed_ids(stream_key, shape, number_of, skew):
    listing = cumulative_ranks(number_of, skew)
    lot = jax.random.randint(jax.random.fold_in(stream_key, 1), shape, 0, int(listing[number_of - 1]))
    rank = jnp.searchsorted(jnp.asarray(listing, jnp.int32), lot, side="right")
    return jax.random.permutation(jax.random.fold_in(stream_key, 2), number_of)[rank].astype(jnp.int32)


def centred(stream_key, extent, deviation, reach, shards=(), kind=jnp.bfloat16):
    factor_of = block_levels(stream_key, extent, shards, -0.22, 0.18) if shards else 1.0
    drawn = jax.random.normal(stream_key, extent, jnp.float32) * deviation * factor_of
    return jnp.minimum(jnp.maximum(drawn, -reach), reach).astype(kind)


def setup_inputs(seed: int = 0) -> dict:
    key_list = jax.random.split(jax.random.key(seed), 7)
    record = centred(key_list[0], (STATIONS, TRACE), 1.0, 6.0, (), jnp.float32)
    shifts = plant(jax.random.randint(key_list[1], (STATIONS, NZ), 0, TRACE - TIMES + 1), jax.random.fold_in(key_list[1], 1), 0, TRACE - TIMES).astype(jnp.int32)
    station_group = plant(skewed_ids(key_list[2], (STATIONS,), GROUPS, 2), jax.random.fold_in(key_list[2], 3), 0, GROUPS - 1).astype(jnp.int32)
    weights = centred(key_list[3], (STATIONS, NX, NY), 1.0, 6.0, ((0, 2), (1, 4)))
    psf_real = centred(key_list[4], (NZ, NX, NY), 1.0, 6.0, ((1, 4), (2, 4)), jnp.float32)
    psf_imag = centred(key_list[5], (NZ, NX, NY), 1.0, 6.0, ((1, 4), (2, 4)), jnp.float32)
    return dict(record=record, shifts=shifts, station_group=station_group, weights=weights, psf_real=psf_real, psf_imag=psf_imag)


NOISE_POWER = 0.25


def station_counts(station_group):
    labels = jnp.arange(GROUPS, dtype=jnp.int32)
    onehot = (station_group[:, None] == labels[None, :]).astype(jnp.float32)
    totals = jnp.sum(onehot, axis=0)
    return jnp.dot(onehot, totals, precision=lax.Precision.HIGHEST)


def coefficients(record, shifts, per_station, first_time, num_times):
    times_range = first_time + jnp.arange(num_times, dtype=jnp.int32)
    positions = (shifts[:, :, None] + times_range[None, None, :]).astype(jnp.int32)
    values = jnp.take_along_axis(record, positions.reshape(positions.shape[0], -1), axis=1)
    scaled = values.reshape(positions.shape) / per_station[:, None, None]
    return jnp.transpose(scaled, (2, 1, 0)).astype(jnp.bfloat16)


def reference(record, shifts, station_group, weights, psf_real, psf_imag):
    per_station = station_counts(station_group)
    coefficient = coefficients(record, shifts, per_station, 0, TIMES)
    stack = jnp.dot(coefficient.reshape(TIMES * NZ, STATIONS), weights.reshape(STATIONS, NX * NY),
                    preferred_element_type=jnp.float32).reshape(TIMES, NZ, NX, NY)
    spectrum = jnp.fft.fftn(stack, axes=(1, 2, 3))
    spec_real = jnp.real(spectrum)
    spec_imag = jnp.imag(spectrum)
    power = psf_real * psf_real + psf_imag * psf_imag + NOISE_POWER
    filt_real = (psf_real * spec_real + psf_imag * spec_imag) / power
    filt_imag = (psf_real * spec_imag - psf_imag * spec_real) / power
    result = jnp.fft.ifftn(filt_real + 1j * filt_imag, axes=(1, 2, 3))
    return jnp.real(result)
```

```python
import functools
import math

import jax
import jax.numpy as jnp
from jax import lax
from jax.experimental import pallas as pl
from jax.experimental.pallas import tpu as pltpu
from jax.sharding import PartitionSpec as P

GROUPS = 8
NOISE_POWER = 0.25
HIGHEST = lax.Precision.HIGHEST
VMEM_BYTES = 50 * 1024 * 1024
BLOCK = 16


def station_counts(station_group):
    labels = jnp.arange(GROUPS, dtype=jnp.int32)
    onehot = (station_group[:, None] == labels[None, :]).astype(jnp.float32)
    totals = jnp.sum(onehot, axis=0)
    return jnp.dot(onehot, totals, precision=HIGHEST)


def coefficients(record, shifts, per_station, time):
    positions = shifts + time
    samples = jnp.arange(record.shape[1], dtype=jnp.int32)
    chosen = jnp.where(
        positions[:, :, None] == samples[None, None, :], record[:, None, :], 0.0
    )
    values = jnp.sum(chosen, axis=2)
    scaled = values / per_station[:, None]
    return jnp.transpose(scaled, (1, 0)).astype(jnp.bfloat16)


def fourier_parts(rows, columns, length, scale):
    angles = (rows[:, None] * columns[None, :] % length).astype(jnp.float32)
    angles = angles * (2.0 * math.pi / length)
    return jnp.cos(angles) * scale, jnp.sin(angles) * scale


def halves(table):
    high = lax.reduce_precision(table, 8, 7)
    return high.astype(jnp.bfloat16), (table - high).astype(jnp.bfloat16)


def dot(a, b):
    return jnp.dot(a, b, preferred_element_type=jnp.float32)


def dot3(high, low, value):
    value_high = value.astype(jnp.bfloat16)
    value_low = (value - value_high.astype(jnp.float32)).astype(jnp.bfloat16)
    return dot(high, value_high) + dot(low, value_high) + dot(high, value_low)


def cost(flops, arrays):
    moved = sum(math.prod(a.shape) * jnp.dtype(a.dtype).itemsize for a in arrays)
    return pl.CostEstimate(flops=flops, bytes_accessed=moved, transcendentals=0)


def whole(array):
    rank = len(array.shape)
    return pl.BlockSpec(array.shape, lambda i: (0,) * rank)


PARAMS = pltpu.CompilerParams(vmem_limit_bytes=VMEM_BYTES)


def lateral_kernel(weights, y_high, y_low, x_high, x_low, out, rest, held):
    parts, stations, rows, width = weights.shape
    bins = out.shape[0]
    half = out.shape[2] // 2
    for s in range(stations):
        piece = weights[:, s, :, :].reshape(parts * rows, width)
        along_y = dot(piece, y_high[...]) + dot(piece, y_low[...])
        both = dot3(x_high[...], x_low[...], along_y)
        cosine, sine = both[:bins], both[bins:]
        held[:, s, :half] = cosine[:, :half] + sine[:, half:]
        held[:, s, half:] = cosine[:, half:] - sine[:, :half]
    value = held[...]
    high = value.astype(out.dtype)
    out[...] = high
    rest[...] = (value - high.astype(jnp.float32)).astype(rest.dtype)


def lateral(weights, y_parts, x_parts):
    parts, stations, rows, width = weights.shape
    bins = x_parts[0].shape[0] // 2
    columns = y_parts[0].shape[1]
    tables = [*y_parts, *x_parts]
    result = jax.ShapeDtypeStruct((bins, stations, columns), jnp.bfloat16)
    spec = pl.BlockSpec((bins, BLOCK, columns), lambda i: (0, i, 0))
    macs = stations * parts * rows * columns * (2 * width + 6 * bins)
    return pl.pallas_call(
        lateral_kernel,
        grid=(stations // BLOCK,),
        in_specs=[
            pl.BlockSpec((parts, BLOCK, rows, width), lambda i: (0, i, 0, 0)),
            *[whole(t) for t in tables],
        ],
        out_specs=[spec, spec],
        out_shape=[result, result],
        scratch_shapes=[pltpu.VMEM((bins, BLOCK, columns), jnp.float32)],
        compiler_params=PARAMS,
        cost_estimate=cost(4 * macs, [weights, result, result]),
        name="lateral",
    )(weights, *tables)


def depth_kernel(pieces, outs, coef, *refs):
    spectra = refs[:pieces]
    psf_real, psf_imag, z_high, z_low = refs[pieces : pieces + 4]
    out_refs, held = refs[pieces + 4 : -1], refs[-1]
    depth, block, half = psf_real.shape
    main = 2 * pieces // 3
    coef_whole = coef[...]
    for b in range(block):
        piece = jnp.concatenate([r[b] for r in spectra[:main]], axis=0)
        rest = jnp.concatenate([r[b] for r in spectra[main:]], axis=0)
        rows = 2 * piece.shape[0]
        both = dot(coef_whole[:, :rows], jnp.concatenate([piece, piece], axis=0))
        both = both + dot(coef_whole[:, rows:], rest)
        real_part, imag_part = both[:depth], both[depth:]
        spec_real = real_part[:, :half] - imag_part[:, half:]
        spec_imag = real_part[:, half:] + imag_part[:, :half]
        p_real, p_imag = psf_real[:, b, :], psf_imag[:, b, :]
        inverse = 1.0 / (p_real * p_real + p_imag * p_imag + NOISE_POWER)
        filt_real = (p_real * spec_real + p_imag * spec_imag) * inverse
        filt_imag = (p_real * spec_imag - p_imag * spec_real) * inverse
        filtered = jnp.concatenate([filt_real, filt_imag], axis=1)
        back = dot3(z_high[...], z_low[...], filtered)
        cosine, sine = back[:depth], back[depth:]
        held[:, b, :half] = cosine[:, :half] - sine[:, half:]
        held[:, b, half:] = cosine[:, half:] + sine[:, :half]
    size = depth // outs
    for k in range(outs):
        out_refs[k][...] = held[k * size : (k + 1) * size].astype(out_refs[k].dtype)


def depth_stage(coef, spectra, psf_real, psf_imag, z_parts, outs, first, bins):
    _, stations, columns = spectra[0].shape
    depth, _, width = psf_real.shape
    block = min(BLOCK, bins)
    skip = first // block
    size = depth // outs
    result = jax.ShapeDtypeStruct((size, bins, columns), jnp.bfloat16)
    psf_spec = pl.BlockSpec((depth, block, width), lambda i: (0, i + skip, 0))
    field = jax.ShapeDtypeStruct((depth, bins, columns), jnp.float32)
    macs = 2 * depth * bins * columns * (coef.shape[1] + 3 * depth)
    return pl.pallas_call(
        functools.partial(depth_kernel, len(spectra), outs),
        grid=(bins // block,),
        in_specs=[
            whole(coef),
            *[
                pl.BlockSpec((block, stations, columns), lambda i: (i + skip, 0, 0))
                for _ in spectra
            ],
            psf_spec,
            psf_spec,
            *[whole(t) for t in z_parts],
        ],
        out_specs=[pl.BlockSpec((size, block, columns), lambda i: (0, i, 0))] * outs,
        out_shape=[result] * outs,
        scratch_shapes=[pltpu.VMEM((depth, block, columns), jnp.float32)],
        compiler_params=PARAMS,
        cost_estimate=cost(4 * macs, [field, field]),
        name="depth",
    )(coef, *spectra, psf_real, psf_imag, *z_parts)


def rows_kernel(pieces, *refs):
    field, (x_high, x_low), outs = refs[:pieces], refs[pieces : pieces + 2], refs[pieces + 2 :]
    block, _, columns = field[0].shape
    half = columns // 2
    length = x_high.shape[1]
    size = length // len(outs)
    for z in range(block):
        piece = jnp.concatenate([f[z] for f in field], axis=0)
        both = dot(x_high[...], piece) + dot(x_low[...], piece)
        cosine, sine = both[:length], both[length:]
        back = jnp.concatenate(
            [cosine[:, :half] - sine[:, half:], cosine[:, half:] + sine[:, :half]], axis=1
        ).astype(jnp.bfloat16)
        for k, out in enumerate(outs):
            out[z] = back[k * size : (k + 1) * size]


def rows_stage(field, x_parts, parts_out):
    slab, bins, columns = field[0].shape
    length = x_parts[0].shape[1]
    block = min(8, slab)
    size = length // parts_out
    result = jax.ShapeDtypeStruct((slab, size, columns), jnp.bfloat16)
    macs = slab * 4 * length * length * columns
    return pl.pallas_call(
        functools.partial(rows_kernel, len(field)),
        grid=(slab // block,),
        in_specs=[
            *[pl.BlockSpec((block, bins, columns), lambda i: (i, 0, 0)) for _ in field],
            *[whole(t) for t in x_parts],
        ],
        out_specs=[pl.BlockSpec((block, size, columns), lambda i: (i, 0, 0))] * parts_out,
        out_shape=[result] * parts_out,
        compiler_params=PARAMS,
        cost_estimate=cost(4 * macs, [*field, *field]),
        name="rows",
    )(*field, *x_parts)


def image_kernel(pieces, *refs):
    field, (y_high, y_low), out = refs[:pieces], refs[pieces : pieces + 2], refs[-1]
    block, rows, columns = field[0].shape
    total = jnp.zeros((block * rows, out.shape[2]), jnp.float32)
    for part in range(pieces):
        piece = field[part][...].reshape(block * rows, columns)
        total = total + dot(piece, y_high[part]) + dot(piece, y_low[part])
    out[...] = total.reshape(out.shape)


def image_stage(field, y_parts, before, first, depth):
    slab, rows, columns = field[0].shape
    block = min(4, slab)
    skip = first // block
    width = y_parts[0].shape[2]
    result = jax.ShapeDtypeStruct((depth, rows, width), jnp.float32)
    held = [] if before is None else [before]
    macs = 2 * slab * rows * columns * len(field) * width
    return pl.pallas_call(
        functools.partial(image_kernel, len(field)),
        grid=(slab // block,),
        in_specs=[
            *[pl.BlockSpec((block, rows, columns), lambda i: (i, 0, 0)) for _ in field],
            *[whole(t) for t in y_parts],
            *[pl.BlockSpec(memory_space=pl.ANY) for _ in held],
        ],
        out_specs=pl.BlockSpec((block, rows, width), lambda i: (i + skip, 0, 0)),
        out_shape=result,
        input_output_aliases={len(field) + 2: 0} if held else {},
        compiler_params=PARAMS,
        cost_estimate=cost(4 * macs, [*field, *field]),
        name="image",
    )(*field, *y_parts, *held)


def from_offset(array, axis, size, offset):
    return lax.ppermute(array, axis, [(i, i ^ offset) for i in range(size)])


def on_device(slabs, parts, record, shifts, station_group, weights, psf_real, psf_imag):
    depth, bins, width = psf_real.shape
    stations = weights.shape[0]
    nx = weights.shape[1] * parts
    ny = weights.shape[2]
    gx, gy, sta = lax.axis_index("gx"), lax.axis_index("gy"), lax.axis_index("sta")
    count = lambda n: jnp.arange(n, dtype=jnp.int32)
    all_x, all_y, all_z = count(nx), count(ny), count(depth)
    own_b = gx * bins + count(bins)
    own_c = gy * width + count(width)
    order_x = [gx ^ k for k in range(slabs)]
    order_y = [gy ^ k for k in range(parts)]

    step = stations // 2
    gathered = [
        lax.all_gather(weights[k * step : (k + 1) * step], "gy", axis=0) for k in range(2)
    ]

    own = coefficients(record, shifts, station_counts(station_group), sta)
    coefficient = lax.all_gather(own, "gx", axis=0, tiled=True).astype(jnp.float32)
    cosine_z, sine_z = fourier_parts(all_z, all_z, depth, 1.0)
    coef_spectrum = jnp.dot(
        jnp.concatenate([cosine_z, -sine_z]), coefficient, precision=HIGHEST
    )
    coef_spectrum = jnp.where(sta == 0, coef_spectrum, jnp.roll(coef_spectrum, stations, axis=1))
    coef_high, coef_low = halves(coef_spectrum)
    coef = jnp.concatenate([coef_high, coef_low, coef_high[:, :stations]], axis=1)
    gathered[0], coef = lax.optimization_barrier((gathered[0], coef))

    cosine_y, sine_y = fourier_parts(all_y, own_c, ny, 1.0)
    cosine_x, sine_x = fourier_parts(own_b, all_x, nx, 1.0)
    y_forward = halves(jnp.concatenate([cosine_y, -sine_y], axis=1))
    x_forward = halves(jnp.concatenate([cosine_x, sine_x], axis=0))
    own_spectra = [lateral(g, y_forward, x_forward) for g in gathered]
    other = [from_offset(high, "sta", 2, 1) for high, _ in own_spectra]
    spectra = [*[high for high, _ in own_spectra], *other, *[low for _, low in own_spectra]]

    slab = depth // slabs
    size = slab // 2
    order_z = jnp.concatenate(
        [p * slab + h * size + count(size) for h in range(2) for p in order_x]
    )
    z_parts = halves(jnp.concatenate(fourier_parts(order_z, all_z, depth, 1.0 / depth)))
    splits = 2 if bins // 2 % BLOCK == 0 else 1
    width_b = bins // splits
    fields = [
        depth_stage(
            coef, spectra, psf_real, psf_imag, z_parts, 2 * slabs, k * width_b, width_b
        )
        for k in range(splits)
    ]

    order_b = jnp.concatenate(
        [p * bins + k * width_b + count(width_b) for k in range(splits) for p in order_x]
    )
    x_rows = jnp.concatenate([p * (nx // parts) + count(nx // parts) for p in order_y])
    x_parts = halves(jnp.concatenate(fourier_parts(x_rows, order_b, nx, 1.0 / nx)))
    cosine_back, sine_back = zip(
        *[fourier_parts(p * width + count(width), all_y, ny, 1.0 / ny) for p in order_y]
    )
    y_parts = halves(
        jnp.stack([jnp.concatenate([c, -s]) for c, s in zip(cosine_back, sine_back)])
    )

    image = None
    arrived = None
    rows = None
    for h in range(2):
        pieces = []
        for k in range(splits):
            sent = list(fields[k][h * slabs : (h + 1) * slabs])
            if arrived is not None:
                if rows is not None and k == splits - 1:
                    sent, arrived, rows = lax.optimization_barrier((sent, arrived, rows))
                else:
                    sent, arrived = lax.optimization_barrier((sent, arrived))
            landed = [sent[0]] + [
                from_offset(sent[p], "gx", slabs, p) for p in range(1, slabs)
            ]
            arrived = landed[1:]
            pieces += landed
        rows = rows_stage(pieces, x_parts, parts)
        ready = [rows[0]] + [from_offset(rows[p], "gy", parts, p) for p in range(1, parts)]
        image = image_stage(ready, y_parts, image, h * size, slab)
    return image[None]


def solution(mesh):
    in_specs = (
        P(),
        P(None, "gx"),
        P(),
        P("sta", "gy", None),
        P(None, "gx", "gy"),
        P(None, "gx", "gy"),
    )
    out_specs = P("sta", "gx", "gy", None)
    return jax.shard_map(
        functools.partial(on_device, mesh.shape["gx"], mesh.shape["gy"]),
        mesh=mesh,
        in_specs=in_specs,
        out_specs=out_specs,
        check_vma=False,
    )
```

```python
import functools
import math

import jax
import jax.numpy as jnp
from jax import lax
from jax.experimental import pallas as pl
from jax.experimental.pallas import tpu as pltpu
from jax.sharding import PartitionSpec as P

GROUPS = 8
NOISE_POWER = 0.25
HIGHEST = lax.Precision.HIGHEST
VMEM_BYTES = 50 * 1024 * 1024
BLOCK = 16


def station_counts(station_group):
    labels = jnp.arange(GROUPS, dtype=jnp.int32)
    onehot = (station_group[:, None] == labels[None, :]).astype(jnp.float32)
    totals = jnp.sum(onehot, axis=0)
    return jnp.dot(onehot, totals, precision=HIGHEST)


def coefficients(record, shifts, per_station, time):
    positions = shifts + time
    samples = jnp.arange(record.shape[1], dtype=jnp.int32)
    chosen = jnp.where(
        positions[:, :, None] == samples[None, None, :], record[:, None, :], 0.0
    )
    values = jnp.sum(chosen, axis=2)
    scaled = values / per_station[:, None]
    return jnp.transpose(scaled, (1, 0)).astype(jnp.bfloat16)


def fourier_parts(rows, columns, length, scale):
    angles = (rows[:, None] * columns[None, :] % length).astype(jnp.float32)
    angles = angles * (2.0 * math.pi / length)
    return jnp.cos(angles) * scale, jnp.sin(angles) * scale


def halves(table):
    high = lax.reduce_precision(table, 8, 7)
    return high.astype(jnp.bfloat16), (table - high).astype(jnp.bfloat16)


def dot(a, b):
    return jnp.dot(a, b, preferred_element_type=jnp.float32)


def dot3(high, low, value):
    value_high = value.astype(jnp.bfloat16)
    value_low = (value - value_high.astype(jnp.float32)).astype(jnp.bfloat16)
    return dot(high, value_high) + dot(low, value_high) + dot(high, value_low)


def cost(flops, arrays):
    moved = sum(math.prod(a.shape) * jnp.dtype(a.dtype).itemsize for a in arrays)
    return pl.CostEstimate(flops=flops, bytes_accessed=moved, transcendentals=0)


def whole(array):
    rank = len(array.shape)
    return pl.BlockSpec(array.shape, lambda i: (0,) * rank)


PARAMS = pltpu.CompilerParams(vmem_limit_bytes=VMEM_BYTES)


def lateral_kernel(weights, y_high, y_low, x_high, x_low, out, rest, held):
    parts, stations, rows, width = weights.shape
    bins = out.shape[0]
    half = out.shape[2] // 2
    for s in range(stations):
        piece = weights[:, s, :, :].reshape(parts * rows, width)
        along_y = dot(piece, y_high[...]) + dot(piece, y_low[...])
        both = dot3(x_high[...], x_low[...], along_y)
        cosine, sine = both[:bins], both[bins:]
        held[:, s, :half] = cosine[:, :half] + sine[:, half:]
        held[:, s, half:] = cosine[:, half:] - sine[:, :half]
    value = held[...]
    high = value.astype(out.dtype)
    out[...] = high
    rest[...] = (value - high.astype(jnp.float32)).astype(rest.dtype)


def lateral(weights, y_parts, x_parts):
    parts, stations, rows, width = weights.shape
    bins = x_parts[0].shape[0] // 2
    columns = y_parts[0].shape[1]
    tables = [*y_parts, *x_parts]
    result = jax.ShapeDtypeStruct((bins, stations, columns), jnp.bfloat16)
    spec = pl.BlockSpec((bins, BLOCK, columns), lambda i: (0, i, 0))
    macs = stations * parts * rows * columns * (2 * width + 6 * bins)
    return pl.pallas_call(
        lateral_kernel,
        grid=(stations // BLOCK,),
        in_specs=[
            pl.BlockSpec((parts, BLOCK, rows, width), lambda i: (0, i, 0, 0)),
            *[whole(t) for t in tables],
        ],
        out_specs=[spec, spec],
        out_shape=[result, result],
        scratch_shapes=[pltpu.VMEM((bins, BLOCK, columns), jnp.float32)],
        compiler_params=PARAMS,
        cost_estimate=cost(4 * macs, [weights, result, result]),
        name="lateral",
    )(weights, *tables)


def depth_kernel(pieces, outs, coef, *refs):
    spectra = refs[:pieces]
    psf_real, psf_imag, z_high, z_low = refs[pieces : pieces + 4]
    out_refs, held = refs[pieces + 4 : -1], refs[-1]
    depth, block, half = psf_real.shape
    main = 2 * pieces // 3
    coef_whole = coef[...]
    for b in range(block):
        piece = jnp.concatenate([r[b] for r in spectra[:main]], axis=0)
        rest = jnp.concatenate([r[b] for r in spectra[main:]], axis=0)
        rows = 2 * piece.shape[0]
        both = dot(coef_whole[:, :rows], jnp.concatenate([piece, piece], axis=0))
        both = both + dot(coef_whole[:, rows:], rest)
        real_part, imag_part = both[:depth], both[depth:]
        spec_real = real_part[:, :half] - imag_part[:, half:]
        spec_imag = real_part[:, half:] + imag_part[:, :half]
        p_real, p_imag = psf_real[:, b, :], psf_imag[:, b, :]
        inverse = 1.0 / (p_real * p_real + p_imag * p_imag + NOISE_POWER)
        filt_real = (p_real * spec_real + p_imag * spec_imag) * inverse
        filt_imag = (p_real * spec_imag - p_imag * spec_real) * inverse
        filtered = jnp.concatenate([filt_real, filt_imag], axis=1)
        back = dot3(z_high[...], z_low[...], filtered)
        cosine, sine = back[:depth], back[depth:]
        held[:, b, :half] = cosine[:, :half] - sine[:, half:]
        held[:, b, half:] = cosine[:, half:] + sine[:, :half]
    size = depth // outs
    for k in range(outs):
        out_refs[k][...] = held[k * size : (k + 1) * size].astype(out_refs[k].dtype)


def depth_stage(coef, spectra, psf_real, psf_imag, z_parts, outs, first, bins):
    _, stations, columns = spectra[0].shape
    depth, _, width = psf_real.shape
    block = min(BLOCK, bins)
    skip = first // block
    size = depth // outs
    result = jax.ShapeDtypeStruct((size, bins, columns), jnp.bfloat16)
    psf_spec = pl.BlockSpec((depth, block, width), lambda i: (0, i + skip, 0))
    field = jax.ShapeDtypeStruct((depth, bins, columns), jnp.float32)
    macs = 2 * depth * bins * columns * (coef.shape[1] + 3 * depth)
    return pl.pallas_call(
        functools.partial(depth_kernel, len(spectra), outs),
        grid=(bins // block,),
        in_specs=[
            whole(coef),
            *[
                pl.BlockSpec((block, stations, columns), lambda i: (i + skip, 0, 0))
                for _ in spectra
            ],
            psf_spec,
            psf_spec,
            *[whole(t) for t in z_parts],
        ],
        out_specs=[pl.BlockSpec((size, block, columns), lambda i: (0, i, 0))] * outs,
        out_shape=[result] * outs,
        scratch_shapes=[pltpu.VMEM((depth, block, columns), jnp.float32)],
        compiler_params=PARAMS,
        cost_estimate=cost(4 * macs, [field, field]),
        name="depth",
    )(coef, *spectra, psf_real, psf_imag, *z_parts)


def rows_kernel(pieces, *refs):
    field, (x_high, x_low), outs = refs[:pieces], refs[pieces : pieces + 2], refs[pieces + 2 :]
    block, _, columns = field[0].shape
    half = columns // 2
    length = x_high.shape[1]
    size = length // len(outs)
    for z in range(block):
        piece = jnp.concatenate([f[z] for f in field], axis=0)
        both = dot(x_high[...], piece) + dot(x_low[...], piece)
        cosine, sine = both[:length], both[length:]
        back = jnp.concatenate(
            [cosine[:, :half] - sine[:, half:], cosine[:, half:] + sine[:, :half]], axis=1
        ).astype(jnp.bfloat16)
        for k, out in enumerate(outs):
            out[z] = back[k * size : (k + 1) * size]


def rows_stage(field, x_parts, parts_out):
    slab, bins, columns = field[0].shape
    length = x_parts[0].shape[1]
    block = min(8, slab)
    size = length // parts_out
    result = jax.ShapeDtypeStruct((slab, size, columns), jnp.bfloat16)
    macs = slab * 4 * length * length * columns
    return pl.pallas_call(
        functools.partial(rows_kernel, len(field)),
        grid=(slab // block,),
        in_specs=[
            *[pl.BlockSpec((block, bins, columns), lambda i: (i, 0, 0)) for _ in field],
            *[whole(t) for t in x_parts],
        ],
        out_specs=[pl.BlockSpec((block, size, columns), lambda i: (i, 0, 0))] * parts_out,
        out_shape=[result] * parts_out,
        compiler_params=PARAMS,
        cost_estimate=cost(4 * macs, [*field, *field]),
        name="rows",
    )(*field, *x_parts)


def image_kernel(pieces, *refs):
    field, (y_high, y_low), out = refs[:pieces], refs[pieces : pieces + 2], refs[-1]
    block, rows, columns = field[0].shape
    total = jnp.zeros((block * rows, out.shape[2]), jnp.float32)
    for part in range(pieces):
        piece = field[part][...].reshape(block * rows, columns)
        total = total + dot(piece, y_high[part]) + dot(piece, y_low[part])
    out[...] = total.reshape(out.shape)


def image_stage(field, y_parts, before, first, depth):
    slab, rows, columns = field[0].shape
    block = min(4, slab)
    skip = first // block
    width = y_parts[0].shape[2]
    result = jax.ShapeDtypeStruct((depth, rows, width), jnp.float32)
    held = [] if before is None else [before]
    macs = 2 * slab * rows * columns * len(field) * width
    return pl.pallas_call(
        functools.partial(image_kernel, len(field)),
        grid=(slab // block,),
        in_specs=[
            *[pl.BlockSpec((block, rows, columns), lambda i: (i, 0, 0)) for _ in field],
            *[whole(t) for t in y_parts],
            *[pl.BlockSpec(memory_space=pl.ANY) for _ in held],
        ],
        out_specs=pl.BlockSpec((block, rows, width), lambda i: (i + skip, 0, 0)),
        out_shape=result,
        input_output_aliases={len(field) + 2: 0} if held else {},
        compiler_params=PARAMS,
        cost_estimate=cost(4 * macs, [*field, *field]),
        name="image",
    )(*field, *y_parts, *held)


def from_offset(array, axis, size, offset):
    return lax.ppermute(array, axis, [(i, i ^ offset) for i in range(size)])


def on_device(slabs, parts, record, shifts, station_group, weights, psf_real, psf_imag):
    depth, bins, width = psf_real.shape
    stations = weights.shape[0]
    nx = weights.shape[1] * parts
    ny = weights.shape[2]
    gx, gy, sta = lax.axis_index("gx"), lax.axis_index("gy"), lax.axis_index("sta")
    count = lambda n: jnp.arange(n, dtype=jnp.int32)
    all_x, all_y, all_z = count(nx), count(ny), count(depth)
    own_b = gx * bins + count(bins)
    own_c = gy * width + count(width)
    order_x = [gx ^ k for k in range(slabs)]
    order_y = [gy ^ k for k in range(parts)]

    step = stations // 2
    gathered = [
        lax.all_gather(weights[k * step : (k + 1) * step], "gy", axis=0) for k in range(2)
    ]

    own = coefficients(record, shifts, station_counts(station_group), sta)
    coefficient = lax.all_gather(own, "gx", axis=0, tiled=True).astype(jnp.float32)
    cosine_z, sine_z = fourier_parts(all_z, all_z, depth, 1.0)
    coef_spectrum = jnp.dot(
        jnp.concatenate([cosine_z, -sine_z]), coefficient, precision=HIGHEST
    )
    coef_spectrum = jnp.where(sta == 0, coef_spectrum, jnp.roll(coef_spectrum, stations, axis=1))
    coef_high, coef_low = halves(coef_spectrum)
    coef = jnp.concatenate([coef_high, coef_low, coef_high[:, :stations]], axis=1)
    gathered[0], coef = lax.optimization_barrier((gathered[0], coef))

    cosine_y, sine_y = fourier_parts(all_y, own_c, ny, 1.0)
    cosine_x, sine_x = fourier_parts(own_b, all_x, nx, 1.0)
    y_forward = halves(jnp.concatenate([cosine_y, -sine_y], axis=1))
    x_forward = halves(jnp.concatenate([cosine_x, sine_x], axis=0))
    own_spectra = [lateral(gathered[0], y_forward, x_forward)]
    gathered[1], own_spectra[0] = lax.optimization_barrier((gathered[1], own_spectra[0]))
    own_spectra.append(lateral(gathered[1], y_forward, x_forward))
    other = [from_offset(high, "sta", 2, 1) for high, _ in own_spectra]
    spectra = [*[high for high, _ in own_spectra], *other, *[low for _, low in own_spectra]]

    slab = depth // slabs
    size = slab // 2
    order_z = jnp.concatenate(
        [p * slab + h * size + count(size) for h in range(2) for p in order_x]
    )
    z_parts = halves(jnp.concatenate(fourier_parts(order_z, all_z, depth, 1.0 / depth)))
    splits = 2 if bins // 2 % BLOCK == 0 else 1
    width_b = bins // splits
    fields = [
        depth_stage(
            coef, spectra, psf_real, psf_imag, z_parts, 2 * slabs, k * width_b, width_b
        )
        for k in range(splits)
    ]

    order_b = jnp.concatenate(
        [p * bins + k * width_b + count(width_b) for k in range(splits) for p in order_x]
    )
    x_rows = jnp.concatenate([p * (nx // parts) + count(nx // parts) for p in order_y])
    x_parts = halves(jnp.concatenate(fourier_parts(x_rows, order_b, nx, 1.0 / nx)))
    cosine_back, sine_back = zip(
        *[fourier_parts(p * width + count(width), all_y, ny, 1.0 / ny) for p in order_y]
    )
    y_parts = halves(
        jnp.stack([jnp.concatenate([c, -s]) for c, s in zip(cosine_back, sine_back)])
    )

    image = None
    arrived = None
    rows = None
    for h in range(2):
        pieces = []
        for k in range(splits):
            sent = list(fields[k][h * slabs : (h + 1) * slabs])
            if arrived is not None:
                if rows is not None and k == splits - 1:
                    sent, arrived, rows = lax.optimization_barrier((sent, arrived, rows))
                else:
                    sent, arrived = lax.optimization_barrier((sent, arrived))
            landed = [sent[0]] + [
                from_offset(sent[p], "gx", slabs, p) for p in range(1, slabs)
            ]
            arrived = landed[1:]
            pieces += landed
        rows = rows_stage(pieces, x_parts, parts)
        ready = [rows[0]] + [from_offset(rows[p], "gy", parts, p) for p in range(1, parts)]
        image = image_stage(ready, y_parts, image, h * size, slab)
    return image[None]


def solution(mesh):
    in_specs = (
        P(),
        P(None, "gx"),
        P(),
        P("sta", "gy", None),
        P(None, "gx", "gy"),
        P(None, "gx", "gy"),
    )
    out_specs = P("sta", "gx", "gy", None)
    return jax.shard_map(
        functools.partial(on_device, mesh.shape["gx"], mesh.shape["gy"]),
        mesh=mesh,
        in_specs=in_specs,
        out_specs=out_specs,
        check_vma=False,
    )
```
